32 devices in a mesh: row: 16 (over z, y, core), col: 2 (over x).
Axes of the slice: x: 2, y: 2, z: 4, core: 2. Of those that a mesh axis runs over, the one named last changes fastest.
Arguments:
- known_inverse: float32 [20480, 20480], P('row', 'col'), may hold values from -1.7818667 to 1.7818667, as said below
- first_panel: float32 [20480, 512], P('col', 'row'), may hold values from -1.25 to 1.25
- second_panel: float32 [20480, 512], P('col', 'row'), may hold values from -1.25 to 1.25
- coupling: float32 [512, 512], replicated, may hold values from -0.25 to 0.25
- first_diag: float32 [512, 512], replicated, may hold values from -6 to 6
- second_diag: float32 [512, 512], replicated, may hold values from -6 to 6
- first_present: int32 [160], replicated, may hold values 0 or 1
- second_present: int32 [160], replicated, may hold values 0 or 1
Outputs:
- first_block: float32 [20480, 512], P(('row', 'col'))
- first_inverse_diag: float32 [512, 512], P(None, 'col')
- second_block: float32 [20480, 512], P(('row', 'col'))
- second_cross: float32 [512, 512], P(None, 'col')
- second_inverse_diag: float32 [512, 512], P(None, 'col')
The draws below stay inside these ranges and needn't reach their ends.
Inputs may be any that keep to these rules, and one draw needn't show every extreme that they name: known_inverse is exactly symmetric.
All inputs are finite; a program needn't handle non-finite values.
Results may differ from the reference program's by a relative error of at most 0.000098.
Values sent between devices are 32-bit elements; how exact they have to be, the bound alone decides.
No kernel may reach another device: no remote copies, remote signals or barrier semaphores. Data moves between devices by JAX's collectives and lax.ppermute only.
A program may use at most 192 MiB of HBM per device.

```python
import jax
import jax.numpy as jnp
from jax import lax

S = 20480
W = 512
BLK = 128
NB = 160


def draw_known_inverse(key, part):
    first_key = jax.random.fold_in(jax.random.fold_in(key, 11), 0)
    base = jnp.clip(jax.random.normal(first_key, (S, S), jnp.float32), -5.0, 5.0)
    result = (base + base.T) * (4.0 / (2.0 * S) ** 0.5)
    return result


def place_ends(entries, rng, low, top_value):
    dims = entries.shape
    spot = [jax.random.randint(jax.random.fold_in(rng, axis), (), 0, dims[axis]) for axis in range(len(dims))]
    entries = entries.at[tuple(spot)].set(low)
    longest = dims.index(max(dims))
    spot[longest] = (spot[longest] + 1) % dims[longest]
    return entries.at[tuple(spot)].set(top_value)


def levels(stream_key, shape, pieces, smallest, largest):
    loudness = 1.0
    for position, blocks in pieces:
        steps = jax.random.uniform(jax.random.fold_in(jax.random.fold_in(stream_key, 6), position), (blocks,), jnp.float32, smallest / len(pieces), largest / len(pieces))
        loudness = loudness * jnp.repeat(jnp.exp(steps), shape[position] // blocks).reshape((-1,) + (1,) * (len(shape) - 1 - position))
    return loudness


def gaussian(stream_key, extent, deviation, reach, cuts=(), kind=jnp.bfloat16):
    drawn = deviation * jax.random.normal(stream_key, extent, jnp.float32)
    if cuts:
        drawn = drawn * levels(stream_key, extent, cuts, -0.22, 0.18)
    return jnp.clip(drawn, -reach, reach).astype(kind)


def setup_inputs(seed: int = 0) -> dict:
    seeds = jax.random.split(jax.random.key(seed), 9)
    known_inverse = draw_known_inverse(jax.random.fold_in(seeds[8], 71), 0)
    first_panel = gaussian(seeds[1], (S, W), (S ** -0.25), 1.25, ((0, 2), (1, 16)), jnp.float32)
    second_panel = gaussian(seeds[2], (S, W), (S ** -0.25), 1.25, ((0, 2), (1, 16)), jnp.float32)
    coupling = gaussian(seeds[3], (W, W), W ** -0.5, 0.25, (), jnp.float32)
    first_diag = gaussian(seeds[4], (W, W), 1.0, 6.0, (), jnp.float32)
    second_diag = gaussian(seeds[5], (W, W), 1.0, 6.0, (), jnp.float32)
    first_present = place_ends((jax.random.randint(seeds[6], (NB,), 0, 2) < 1).astype(jnp.int32), jax.random.fold_in(seeds[6], 1), 0, 1)
    second_present = place_ends((jax.random.randint(seeds[7], (NB,), 0, 2) < 1).astype(jnp.int32), jax.random.fold_in(seeds[7], 1), 0, 1)
    return {"known_inverse": known_inverse, "first_panel": first_panel, "second_panel": second_panel, "coupling": coupling, "first_diag": first_diag, "second_diag": second_diag, "first_present": first_present, "second_present": second_present}


def product(left, right):
    return jnp.dot(left, right, precision=lax.Precision.HIGHEST, preferred_element_type=jnp.float32)


def present_rows(present):
    return jnp.repeat(present.astype(jnp.float32), BLK)[:, None]


def reference(known_inverse, first_panel, second_panel, coupling, first_diag, second_diag, first_present, second_present):
    panel_one = first_panel * present_rows(first_present)
    panel_two = second_panel * present_rows(second_present)
    first_block = -product(known_inverse, panel_one)
    first_inverse_diag = first_diag - product(panel_one.T, first_block)
    second_block = -(product(known_inverse, panel_two) + product(first_block, coupling))
    second_cross = -(product(first_block.T, panel_two) + product(first_inverse_diag, coupling))
    second_inverse_diag = second_diag - product(panel_two.T, second_block) - product(coupling.T, second_cross)
    return first_block, first_inverse_diag, second_block, second_cross, second_inverse_diag
```

```python
import functools

import jax
import jax.numpy as jnp
from jax import lax
from jax.experimental import pallas as pl
from jax.experimental.pallas import tpu as pltpu
from jax.sharding import PartitionSpec as P

BLK = 128
GROUP = 4
SLOTS = 3
VMEM_BYTES = 50 * 2**20
LEVELS = (0.55, 0.6, 1.0)
BF16 = jnp.bfloat16


def product(left, right):
    return jnp.dot(left, right, precision=lax.Precision.HIGHEST, preferred_element_type=jnp.float32)


def transposed(left, right):
    return lax.dot_general(
        left,
        right,
        (((0,), (0,)), ((), ())),
        precision=lax.Precision.HIGHEST,
        preferred_element_type=jnp.float32,
    )


def masked(panel, present, col_index):
    row_total, col_total = panel.shape
    blocks = row_total // BLK
    local = lax.dynamic_slice_in_dim(present, col_index * blocks, blocks)
    shaped = panel.reshape(blocks, BLK, col_total) * local.astype(jnp.float32)[:, None, None]
    return shaped.reshape(row_total, col_total)


def piece_products(known_inverse, column_one, column_two, piece_one, piece_two, coupling):
    first_block = -lax.psum_scatter(
        product(known_inverse, column_one), "col", scatter_dimension=0, tiled=True
    )
    reached = lax.psum_scatter(
        product(known_inverse, column_two), "col", scatter_dimension=0, tiled=True
    )
    first_partial = transposed(piece_one, first_block)
    second_block = -(reached + product(first_block, coupling))
    cross_partial = transposed(first_block, piece_two)
    diag_partial = transposed(piece_two, second_block)
    return (first_block, second_block, first_partial, cross_partial, diag_partial)


def dense(
    known_inverse,
    first_panel,
    second_panel,
    coupling,
    first_diag,
    second_diag,
    first_present,
    second_present,
):
    col_count = lax.axis_size("col")
    row_index = lax.axis_index("row")
    col_index = lax.axis_index("col")
    local_one = masked(first_panel, first_present, col_index)
    local_two = masked(second_panel, second_present, col_index)
    column_one, column_two = (
        lax.all_gather(local_one, "row", axis=1, tiled=True),
        lax.all_gather(local_two, "row", axis=1, tiled=True),
    )
    band_rows = known_inverse.shape[0]
    block_cols = known_inverse.shape[1]
    width_total = coupling.shape[0]
    owner = row_index * band_rows // block_cols
    offset = row_index * band_rows % block_cols
    is_owner = (col_index == owner).astype(jnp.float32)
    band_one = lax.dynamic_slice_in_dim(column_one, offset, band_rows) * is_owner
    band_two = lax.dynamic_slice_in_dim(column_two, offset, band_rows) * is_owner
    piece_one, piece_two = (
        lax.psum_scatter(band_one, "col", scatter_dimension=0, tiled=True),
        lax.psum_scatter(band_two, "col", scatter_dimension=0, tiled=True),
    )
    first_block, second_block, first_partial, cross_partial, diag_partial = piece_products(
        known_inverse, column_one, column_two, piece_one, piece_two, coupling
    )
    col_width = width_total // col_count
    col_start = col_index * col_width
    first_sum = lax.psum(first_partial, ("row", "col"))
    first_inverse_diag = first_diag - first_sum
    cross_sum, diag_sum = lax.psum((cross_partial, diag_partial), ("row", "col"))
    second_cross = -(cross_sum + product(first_inverse_diag, coupling))
    second_inverse_diag = second_diag - diag_sum - transposed(coupling, second_cross)
    first_out = lax.dynamic_slice_in_dim(first_inverse_diag, col_start, col_width, 1)
    cross_out = lax.dynamic_slice_in_dim(second_cross, col_start, col_width, 1)
    second_out = lax.dynamic_slice_in_dim(second_inverse_diag, col_start, col_width, 1)
    return (first_block, first_out, second_block, cross_out, second_out)


def near(left, right, dims=(((1,), (0,)), ((), ()))):
    return lax.dot_general(left, right, dims, precision=lax.Precision.HIGH, preferred_element_type=jnp.float32)


def in_smem():
    return pl.BlockSpec(memory_space=pltpu.SMEM)


def in_vmem():
    return pl.BlockSpec(memory_space=pltpu.VMEM)


def lanes(start):
    return pl.ds(pl.multiple_of(start * BLK, BLK), BLK)


def split(value):
    high = value.astype(BF16)
    return high, (value - high.astype(jnp.float32)).astype(BF16)


def present_rows(one, two, panel_one, panel_two, capacity):
    width, total = panel_one.shape
    blocks = total // BLK

    def kernel(one_ref, two_ref, first_ref, second_ref, out_ref, list_ref, at_one, at_two, by_one, by_two, size_ref):
        def body(block, carry):
            place, size = carry
            for present_ref, source, at_ref, by_ref in (
                (one_ref, first_ref, at_one, by_one),
                (two_ref, second_ref, at_two, by_two),
            ):
                here = present_ref[block]
                spot = jnp.where(here > 0, place, -1)
                at_ref[size] = spot
                by_ref[block] = spot

                @pl.when(jnp.logical_and(here > 0, place < capacity))
                def _(place=place, source=source):
                    out_ref[:, lanes(place)] = source[:, lanes(block)]

                place = place + here
            list_ref[size] = block
            return place, size + jnp.maximum(one_ref[block], two_ref[block])

        place, size = lax.fori_loop(0, blocks, body, (jnp.int32(0), jnp.int32(0)))
        size_ref[0] = size

        def rest(entry, _):
            list_ref[entry] = 0
            at_one[entry] = -1
            at_two[entry] = -1
            return 0

        lax.fori_loop(size, blocks, rest, 0)

        def clear(entry, _):
            out_ref[:, lanes(entry)] = jnp.zeros((width, BLK), jnp.float32)
            return 0

        lax.fori_loop(jnp.minimum(place, capacity), capacity, clear, 0)

    ints = jax.ShapeDtypeStruct((blocks,), jnp.int32)
    return pl.pallas_call(
        kernel,
        in_specs=[in_smem(), in_smem(), in_vmem(), in_vmem()],
        out_specs=[in_vmem()] + [in_smem()] * 6,
        out_shape=[
            jax.ShapeDtypeStruct((width, capacity * BLK), jnp.float32),
            ints,
            ints,
            ints,
            ints,
            ints,
            jax.ShapeDtypeStruct((1,), jnp.int32),
        ],
        compiler_params=pltpu.CompilerParams(vmem_limit_bytes=VMEM_BYTES),
        cost_estimate=pl.CostEstimate(flops=0, transcendentals=0, bytes_accessed=20 * 2**20),
        name="present_rows",
    )(one, two, panel_one, panel_two)


def panel_product(known_inverse, sources, places, band, side, whole):
    block_list, at_one, at_two, by_one, by_two, size = places
    rows, total = known_inverse.shape
    half = rows // 2
    shares = 2 if whole else 1
    widths = [source.shape[0] for source in sources]
    width = sum(widths)
    starts = [sum(widths[:i]) for i in range(len(widths))]
    depth = GROUP * BLK
    count = len(sources)
    outs = 2 * shares if whole else 3

    def kernel(where_ref, size_ref, list_ref, one_ref, two_ref, by_one_ref, by_two_ref, known_ref, *refs):
        source_any, out_refs = refs[:count], refs[count : count + outs]
        source_refs = refs[count + outs : 2 * count + outs]
        slots, right, fetched, arrived = refs[2 * count + outs :]
        products, pieces = out_refs[:shares], out_refs[shares:]
        steps = (size_ref[0] + GROUP - 1) // GROUP
        parts = (1 - where_ref[0], where_ref[0])

        def fetch(step, slot):
            return [
                pltpu.make_async_copy(
                    known_ref.at[pl.ds(pl.multiple_of(parts[p] * half, half), half), lanes(list_ref[step * GROUP + g])],
                    slots.at[slot, p * half : (p + 1) * half, g * BLK : (g + 1) * BLK],
                    fetched.at[slot, p, g],
                )
                for g in range(GROUP)
                for p in range(shares)
            ]

        for ahead in range(SLOTS - 1):

            @pl.when(ahead < steps)
            def _(ahead=ahead):
                for copy in fetch(ahead, ahead):
                    copy.start()

        moves = [pltpu.make_async_copy(source_any[i], source_refs[i], arrived.at[i]) for i in range(count)]
        for move in moves:
            move.start()
        for product in products:
            product[...] = jnp.zeros_like(product)
        for move in moves:
            move.wait()

        for p, piece in enumerate(pieces):
            for panel, by_ref in enumerate((by_one_ref, by_two_ref)):
                for block in range(half // BLK):
                    spot = by_ref[where_ref[1] + parts[p] * (half // BLK) + block]
                    for source, start, height in zip(source_refs, starts, widths):
                        row = panel * width + start
                        value = source[:, lanes(jnp.maximum(spot, 0))]
                        piece[row : row + height, block * BLK : (block + 1) * BLK] = jnp.where(
                            spot >= 0, value, 0.0
                        )

        def times(left, other):
            return lax.dot_general(left, other, (((1,), (1,)), ((), ())), preferred_element_type=jnp.float32)

        def body(step, _):
            slot = lax.rem(step, SLOTS)
            later = step + SLOTS - 1

            @pl.when(later < steps)
            def _():
                for copy in fetch(later, lax.rem(later, SLOTS)):
                    copy.start()

            for g in range(GROUP):
                entry = step * GROUP + g
                for panel, at_ref in enumerate((one_ref, two_ref)):
                    spot = at_ref[entry]
                    keep = jnp.logical_and(spot >= 0, entry < size_ref[0])
                    for source, start, height in zip(source_refs, starts, widths):
                        row = panel * width + start
                        value = source[:, lanes(jnp.maximum(spot, 0))]
                        high, low = split(jnp.where(keep, value, 0.0))
                        right[row : row + height, g * BLK : (g + 1) * BLK] = high
                        right[2 * width + row : 2 * width + row + height, g * BLK : (g + 1) * BLK] = low
            for copy in fetch(step, slot):
                copy.wait()
            high, low = split(slots[slot])
            both = times(high, right[...])
            both = both[:, : 2 * width] + both[:, 2 * width :] + times(low, right[: 2 * width, :])
            for p, product in enumerate(products):
                product[...] += both[p * half : (p + 1) * half]
            return 0

        lax.fori_loop(0, steps, body, 0)

    anywhere = pl.BlockSpec(memory_space=pl.ANY)
    product = jax.ShapeDtypeStruct((half, 2 * width), jnp.float32)
    piece = jax.ShapeDtypeStruct((2 * width, half), jnp.float32)
    where = jnp.stack([side, band]).astype(jnp.int32)
    return pl.pallas_call(
        kernel,
        in_specs=[in_smem()] * 7 + [anywhere] * (1 + count),
        out_specs=[in_vmem()] * outs,
        out_shape=[product] * shares + [piece] * 2,
        scratch_shapes=[pltpu.VMEM(source.shape, jnp.float32) for source in sources]
        + [
            pltpu.VMEM((SLOTS, shares * half, depth), jnp.float32),
            pltpu.VMEM((4 * width, depth), BF16),
            pltpu.SemaphoreType.DMA((SLOTS, shares, GROUP)),
            pltpu.SemaphoreType.DMA((count,)),
        ],
        compiler_params=pltpu.CompilerParams(vmem_limit_bytes=VMEM_BYTES),
        cost_estimate=pl.CostEstimate(
            flops=3 * shares * half * total * width * 2 * 2,
            transcendentals=0,
            bytes_accessed=shares * half * total * 3,
        ),
        name="panel_product",
    )(where, size, block_list, at_one, at_two, by_one, by_two, known_inverse, *sources)


def fold(groups, matrix, before):
    arrays, firsts, heights = [], [], []
    for mine, arrived, sources in groups:
        arrays += [mine, arrived]
        firsts += [first for _, first in sources]
        heights.append([array.shape[0] for array, _ in sources])
    rows = arrays[0].shape[0]
    total = matrix.shape[0] // 2
    count = len(arrays)
    has = before is not None

    def kernel(first_ref, *refs):
        ins, matrix_ref, out_ref = refs[:count], refs[count], refs[-1]

        def times(left, other):
            return lax.dot_general(left, other, (((1,), (0,)), ((), ())), preferred_element_type=jnp.float32)

        value = refs[count + 1][...] if has else None
        entry = 0
        for index, widths in enumerate(heights):
            parts = [
                matrix_ref[pl.ds(pl.multiple_of(panel * total + first_ref[entry + i], 32), w), :]
                for panel in range(2)
                for i, w in enumerate(widths)
            ]
            entry += len(widths)
            big, small = split(jnp.concatenate(parts, axis=0))
            high, low = split(ins[2 * index][...] + ins[2 * index + 1][...])
            part = times(high, big) + times(high, small) + times(low, big)
            value = part if value is None else value + part
        out_ref[...] = value

    return pl.pallas_call(
        kernel,
        in_specs=[in_smem()] + [in_vmem()] * (count + 1 + has),
        out_specs=in_vmem(),
        out_shape=jax.ShapeDtypeStruct((rows, 2 * total), jnp.float32),
        compiler_params=pltpu.CompilerParams(vmem_limit_bytes=VMEM_BYTES),
        cost_estimate=pl.CostEstimate(
            flops=6 * rows * 2 * total * sum(a.shape[1] for a in arrays[::2]),
            transcendentals=0,
            bytes_accessed=8 * rows * total * 2,
        ),
        name="fold",
    )(jnp.stack(firsts).astype(jnp.int32), *arrays, matrix, *([before] if has else []))


def own_rows(pieces, is_owner, total):
    arrays, firsts, heights = [], [], []
    for own, arrived, sources in pieces:
        arrays += [own, arrived]
        firsts += [first for _, first in sources]
        heights.append([array.shape[0] for array, _ in sources])
    count = len(arrays)
    length = arrays[0].shape[1]

    def kernel(first_ref, *refs):
        ins, outs = refs[:count], refs[count:]
        entry = 0
        for index, widths in enumerate(heights):
            here, there = ins[2 * index], ins[2 * index + 1]
            row = 0
            for panel, out in enumerate(outs):
                for i, w in enumerate(widths):
                    value = jnp.where(first_ref[0] > 0, here[row : row + w, :], there[row : row + w, :])
                    out[pl.ds(pl.multiple_of(first_ref[1 + entry + i], 32), w), :] = value
                    row += w
            entry += len(widths)

    return pl.pallas_call(
        kernel,
        in_specs=[in_smem()] + [in_vmem()] * count,
        out_specs=[in_vmem()] * 2,
        out_shape=[jax.ShapeDtypeStruct((total, length), jnp.float32)] * 2,
        compiler_params=pltpu.CompilerParams(vmem_limit_bytes=VMEM_BYTES),
        cost_estimate=pl.CostEstimate(flops=0, transcendentals=0, bytes_accessed=12 * total * length),
        name="own_rows",
    )(jnp.stack([is_owner] + firsts).astype(jnp.int32), *arrays)


def pairs(count, bit):
    return [(i, i ^ bit) for i in range(count)]


def halves(value, dim, side):
    size = value.shape[dim] // 2
    return (
        lax.dynamic_slice_in_dim(value, side * size, size, dim),
        lax.dynamic_slice_in_dim(value, (1 - side) * size, size, dim),
    )


def summed(value, stages):
    kept = []
    for axis, bit in stages:
        count = lax.axis_size(axis)
        side = lax.axis_index(axis) // bit % 2
        mine, theirs = halves(value, 1 if axis == "col" else 0, side)
        value = mine + lax.ppermute(theirs, axis, pairs(count, bit))
        if axis == "row":
            kept.append((bit, side))
    for bit, side in reversed(kept):
        other = lax.ppermute(value, "row", pairs(lax.axis_size("row"), bit))
        value = jnp.where(
            side == 0, jnp.concatenate([value, other], axis=0), jnp.concatenate([other, value], axis=0)
        )
    return value


def ring_chip(position, chips):
    half = chips // 2
    return jnp.where(position < half, 2 * position, 2 * (chips - 1 - position) + 1)


def sparse(
    known_inverse,
    first_panel,
    second_panel,
    coupling,
    first_diag,
    second_diag,
    first_present,
    second_present,
    capacity,
):
    rows = lax.axis_size("row")
    row_index = lax.axis_index("row")
    col_index = lax.axis_index("col")
    band_rows, block_cols = known_inverse.shape
    width = first_panel.shape[1]
    total = coupling.shape[0]
    part_rows = band_rows // 2
    blocks = block_cols // BLK
    chips = rows // 2
    reach = chips // 2
    core = row_index % 2
    chip = row_index // 2
    position = jnp.where(chip % 2 == 0, chip // 2, chips - 1 - chip // 2)
    order = [2 * p for p in range(reach)] + [2 * p + 1 for p in reversed(range(reach))]

    own, block_list, at_one, at_two, by_one, by_two, size = present_rows(
        lax.dynamic_slice_in_dim(first_present, col_index * blocks, blocks),
        lax.dynamic_slice_in_dim(second_present, col_index * blocks, blocks),
        first_panel.T,
        second_panel.T,
        capacity,
    )
    places = (block_list, at_one, at_two, by_one, by_two, size)
    owner = row_index * band_rows // block_cols
    band = row_index * band_rows % block_cols // BLK
    to_other = []
    for r in range(rows):
        o = r * band_rows // block_cols
        to_other.append((2 * r + o, 2 * r + 1 - o))
    ring = []
    for p in range(chips):
        ring.append((2 * order[p], 2 * order[(p + 1) % chips]))
        ring.append((2 * order[p] + 1, 2 * order[(p - 1) % chips] + 1))

    def swap(value):
        return lax.ppermute(value, "row", pairs(rows, 1))

    def start(distance):
        return 2 * width * ring_chip((position + distance) % chips, chips)

    identity = jnp.eye(total, dtype=jnp.float32)
    matrix = jnp.concatenate(
        [
            jnp.concatenate([-identity, coupling], axis=1),
            jnp.concatenate([jnp.zeros_like(identity), -identity], axis=1),
        ],
        axis=0,
    )

    other = swap(own)
    moving = jnp.where(core == 0, jnp.concatenate([own, other]), jnp.concatenate([other, own]))
    way = jnp.where(core == 0, -1, 1)
    products, pieces = [], []
    for distance in range(reach + 1):
        last = distance == reach
        if distance == 0:
            sources = [(moving, start(0))]
        elif last:
            shift = jnp.where(core == 0, 0, width)
            sources = [(moving, start(distance) + shift), (swap(moving), start(distance) + width - shift)]
        else:
            sources = [(moving, start(way * distance)), (swap(moving), start(-way * distance))]
        if not last:
            if distance + 1 == reach:
                moving = jnp.where(core == 0, moving[:width], moving[width:])
            moving = lax.ppermute(moving, "row", ring)
        arrays = [array for array, _ in sources]
        if last:
            theirs, other_piece, own_piece = panel_product(known_inverse, arrays, places, band, col_index, False)
        else:
            theirs, mine, other_piece, own_piece = panel_product(
                known_inverse, arrays, places, band, col_index, True
            )
            before = (products[-1][1], pieces[-1][1]) if products else ()
            moving, theirs, other_piece, *before = lax.optimization_barrier((moving, theirs, other_piece, *before))
            if before:
                products[-1] = (products[-1][0], before[0], products[-1][2])
                pieces[-1] = (pieces[-1][0], before[1], pieces[-1][2])
        arrived = lax.ppermute(theirs, "col", pairs(2, 1))
        arrived_piece = lax.ppermute(other_piece, ("row", "col"), to_other)
        if last:
            *arrays, crossed, crossed_piece = lax.optimization_barrier((*arrays, products[-1][1], pieces[-1][1]))
            products[-1] = (products[-1][0], crossed, products[-1][2])
            pieces[-1] = (pieces[-1][0], crossed_piece, pieces[-1][2])
            mine, _, _ = panel_product(known_inverse, arrays, places, band, 1 - col_index, False)
        products.append((mine, arrived, sources))
        pieces.append((own_piece, arrived_piece, sources))

    blocks_out = fold(products[-1:], matrix, fold(products[:-1], matrix, None))
    first_block, second_block = blocks_out[:, :total], blocks_out[:, total:]
    rows_one, rows_two = own_rows(pieces, (col_index == owner).astype(jnp.int32), total)
    rows_two = rows_two - near(coupling, rows_one, (((0,), (0,)), ((), ())))
    sums = (-near(rows_one, first_block), -near(rows_one, second_block), -near(rows_two, second_block))
    bits = []
    bit = 2
    while bit < rows:
        bits.append(("row", bit))
        bit *= 2
    ways = [("col", 1)] + bits
    sums = [
        summed(value, [("row", 1)] + ways[turn % len(ways) :] + ways[: turn % len(ways)])
        for turn, value in enumerate(sums)
    ]
    col_width = total // 2

    def own_columns(value):
        return lax.dynamic_slice_in_dim(value, col_index * col_width, col_width, 1)

    moved = near(first_diag, own_columns(coupling))
    first_out = own_columns(first_diag) + sums[0]
    cross_out = sums[1] - moved
    second_out = own_columns(second_diag) + near(coupling, moved, (((0,), (0,)), ((), ()))) + sums[2]
    return first_block, first_out, second_block, cross_out, second_out


def on_device(*args):
    known_inverse, first_panel, second_panel, coupling = args[:4]
    first_present, second_present = args[6:]
    rows, cols = lax.axis_size("row"), lax.axis_size("col")
    band_rows, block_cols = known_inverse.shape
    width = first_panel.shape[1]
    fits = (
        cols == 2
        and rows >= 4
        and rows & (rows - 1) == 0
        and band_rows % (2 * BLK) == 0
        and block_cols % (band_rows) == 0
        and block_cols % (GROUP * BLK) == 0
        and width % 32 == 0
        and coupling.shape[0] % (2 * 16 * rows) == 0
    )
    if not fits:
        return dense(*args)
    blocks = block_cols // BLK
    counts = (first_present + second_present).reshape(cols, blocks).sum(axis=1)
    capacities = [int(share * 2 * blocks) for share in LEVELS]
    level = sum((jnp.max(counts) > capacity).astype(jnp.int32) for capacity in capacities[:-1])
    branches = [functools.partial(sparse, capacity=capacity) for capacity in capacities]
    return lax.switch(level, branches, *args)


def solution(mesh):
    in_specs = (P("row", "col"), P("col", "row"), P("col", "row"), P(), P(), P(), P(), P())
    out_specs = (
        P(("row", "col"), None),
        P(None, "col"),
        P(("row", "col"), None),
        P(None, "col"),
        P(None, "col"),
    )
    return jax.shard_map(
        on_device, mesh=mesh, in_specs=in_specs, out_specs=out_specs, check_vma=False
    )
```

```python
import functools

import jax
import jax.numpy as jnp
from jax import lax
from jax.experimental import pallas as pl
from jax.experimental.pallas import tpu as pltpu
from jax.sharding import PartitionSpec as P

BLK = 128
GROUP = 4
SLOTS = 3
VMEM_BYTES = 50 * 2**20
LEVELS = (0.55, 0.6, 1.0)
BF16 = jnp.bfloat16


def product(left, right):
    return jnp.dot(left, right, precision=lax.Precision.HIGHEST, preferred_element_type=jnp.float32)


def transposed(left, right):
    return lax.dot_general(
        left,
        right,
        (((0,), (0,)), ((), ())),
        precision=lax.Precision.HIGHEST,
        preferred_element_type=jnp.float32,
    )


def masked(panel, present, col_index):
    row_total, col_total = panel.shape
    blocks = row_total // BLK
    local = lax.dynamic_slice_in_dim(present, col_index * blocks, blocks)
    shaped = panel.reshape(blocks, BLK, col_total) * local.astype(jnp.float32)[:, None, None]
    return shaped.reshape(row_total, col_total)


def piece_products(known_inverse, column_one, column_two, piece_one, piece_two, coupling):
    first_block = -lax.psum_scatter(
        product(known_inverse, column_one), "col", scatter_dimension=0, tiled=True
    )
    reached = lax.psum_scatter(
        product(known_inverse, column_two), "col", scatter_dimension=0, tiled=True
    )
    first_partial = transposed(piece_one, first_block)
    second_block = -(reached + product(first_block, coupling))
    cross_partial = transposed(first_block, piece_two)
    diag_partial = transposed(piece_two, second_block)
    return (first_block, second_block, first_partial, cross_partial, diag_partial)


def dense(
    known_inverse,
    first_panel,
    second_panel,
    coupling,
    first_diag,
    second_diag,
    first_present,
    second_present,
):
    col_count = lax.axis_size("col")
    row_index = lax.axis_index("row")
    col_index = lax.axis_index("col")
    local_one = masked(first_panel, first_present, col_index)
    local_two = masked(second_panel, second_present, col_index)
    column_one, column_two = (
        lax.all_gather(local_one, "row", axis=1, tiled=True),
        lax.all_gather(local_two, "row", axis=1, tiled=True),
    )
    band_rows = known_inverse.shape[0]
    block_cols = known_inverse.shape[1]
    width_total = coupling.shape[0]
    owner = row_index * band_rows // block_cols
    offset = row_index * band_rows % block_cols
    is_owner = (col_index == owner).astype(jnp.float32)
    band_one = lax.dynamic_slice_in_dim(column_one, offset, band_rows) * is_owner
    band_two = lax.dynamic_slice_in_dim(column_two, offset, band_rows) * is_owner
    piece_one, piece_two = (
        lax.psum_scatter(band_one, "col", scatter_dimension=0, tiled=True),
        lax.psum_scatter(band_two, "col", scatter_dimension=0, tiled=True),
    )
    first_block, second_block, first_partial, cross_partial, diag_partial = piece_products(
        known_inverse, column_one, column_two, piece_one, piece_two, coupling
    )
    col_width = width_total // col_count
    col_start = col_index * col_width
    first_sum = lax.psum(first_partial, ("row", "col"))
    first_inverse_diag = first_diag - first_sum
    cross_sum, diag_sum = lax.psum((cross_partial, diag_partial), ("row", "col"))
    second_cross = -(cross_sum + product(first_inverse_diag, coupling))
    second_inverse_diag = second_diag - diag_sum - transposed(coupling, second_cross)
    first_out = lax.dynamic_slice_in_dim(first_inverse_diag, col_start, col_width, 1)
    cross_out = lax.dynamic_slice_in_dim(second_cross, col_start, col_width, 1)
    second_out = lax.dynamic_slice_in_dim(second_inverse_diag, col_start, col_width, 1)
    return (first_block, first_out, second_block, cross_out, second_out)


def near(left, right, dims=(((1,), (0,)), ((), ()))):
    return lax.dot_general(left, right, dims, precision=lax.Precision.HIGH, preferred_element_type=jnp.float32)


def in_smem():
    return pl.BlockSpec(memory_space=pltpu.SMEM)


def in_vmem():
    return pl.BlockSpec(memory_space=pltpu.VMEM)


def lanes(start):
    return pl.ds(pl.multiple_of(start * BLK, BLK), BLK)


def split(value):
    high = value.astype(BF16)
    return high, (value - high.astype(jnp.float32)).astype(BF16)


def present_rows(first, one, two, panel_one, panel_two, capacity):
    width, total = panel_one.shape
    blocks = total // BLK

    def kernel(at_ref, one_ref, two_ref, first_ref, second_ref, out_ref, list_ref, at_one, at_two, by_one, by_two, size_ref):
        def body(block, carry):
            place, size = carry
            either = jnp.int32(0)
            for present_ref, source, entry_ref, by_ref in (
                (one_ref, first_ref, at_one, by_one),
                (two_ref, second_ref, at_two, by_two),
            ):
                here = present_ref[at_ref[0] + block]
                either = jnp.maximum(either, here)
                spot = jnp.where(here > 0, place, -1)
                entry_ref[size] = spot
                by_ref[block] = spot

                @pl.when(jnp.logical_and(here > 0, place < capacity))
                def _(place=place, source=source):
                    out_ref[:, lanes(place)] = source[:, lanes(block)]

                place = place + here
            list_ref[size] = block
            return place, size + either

        place, size = lax.fori_loop(0, blocks, body, (jnp.int32(0), jnp.int32(0)))
        size_ref[0] = size

        def rest(entry, _):
            list_ref[entry] = 0
            at_one[entry] = -1
            at_two[entry] = -1
            return 0

        lax.fori_loop(size, blocks, rest, 0)

        def clear(entry, _):
            out_ref[:, lanes(entry)] = jnp.zeros((width, BLK), jnp.float32)
            return 0

        lax.fori_loop(jnp.minimum(place, capacity), capacity, clear, 0)

    ints = jax.ShapeDtypeStruct((blocks,), jnp.int32)
    return pl.pallas_call(
        kernel,
        in_specs=[in_smem()] * 3 + [in_vmem()] * 2,
        out_specs=[in_vmem()] + [in_smem()] * 6,
        out_shape=[
            jax.ShapeDtypeStruct((width, capacity * BLK), jnp.float32),
            ints,
            ints,
            ints,
            ints,
            ints,
            jax.ShapeDtypeStruct((1,), jnp.int32),
        ],
        compiler_params=pltpu.CompilerParams(vmem_limit_bytes=VMEM_BYTES),
        cost_estimate=pl.CostEstimate(flops=0, transcendentals=0, bytes_accessed=20 * 2**20),
        name="present_rows",
    )(first, one, two, panel_one, panel_two)


def band_rows_of(sources, by_one, by_two, band, side, half):
    widths = [source.shape[0] for source in sources]
    width = sum(widths)
    starts = [sum(widths[:i]) for i in range(len(widths))]
    count = len(sources)

    def kernel(where_ref, one_ref, two_ref, *refs):
        ins, outs = refs[:count], refs[count:]
        parts = (1 - where_ref[0], where_ref[0])
        for panel, by_ref in enumerate((one_ref, two_ref)):
            for p, out in enumerate(outs):
                for block in range(half // BLK):
                    spot = by_ref[where_ref[1] + parts[p] * (half // BLK) + block]
                    for source, start, height in zip(ins, starts, widths):
                        row = panel * width + start
                        value = source[:, lanes(jnp.maximum(spot, 0))]
                        out[row : row + height, block * BLK : (block + 1) * BLK] = jnp.where(spot >= 0, value, 0.0)

    return pl.pallas_call(
        kernel,
        in_specs=[in_smem()] * 3 + [in_vmem()] * count,
        out_specs=[in_vmem()] * 2,
        out_shape=[jax.ShapeDtypeStruct((2 * width, half), jnp.float32)] * 2,
        compiler_params=pltpu.CompilerParams(vmem_limit_bytes=VMEM_BYTES),
        cost_estimate=pl.CostEstimate(flops=0, transcendentals=0, bytes_accessed=10 * 2**20),
        name="band_rows",
    )(jnp.stack([side, band]).astype(jnp.int32), by_one, by_two, *sources)


def panel_product(known_inverse, sources, places, side):
    block_list, at_one, at_two, size = places
    rows, total = known_inverse.shape
    half = rows // 2
    shares = 2
    widths = [source.shape[0] for source in sources]
    width = sum(widths)
    starts = [sum(widths[:i]) for i in range(len(widths))]
    depth = GROUP * BLK
    count = len(sources)
    outs = shares

    def kernel(where_ref, size_ref, list_ref, one_ref, two_ref, known_ref, *refs):
        source_any, out_refs = refs[:count], refs[count : count + outs]
        source_refs = refs[count + outs : 2 * count + outs]
        slots, right, fetched, arrived = refs[2 * count + outs :]
        steps = (size_ref[0] + GROUP - 1) // GROUP
        parts = (1 - where_ref[0], where_ref[0])

        def fetch(step, slot):
            return [
                pltpu.make_async_copy(
                    known_ref.at[pl.ds(pl.multiple_of(parts[p] * half, half), half), lanes(list_ref[step * GROUP + g])],
                    slots.at[slot, p * half : (p + 1) * half, g * BLK : (g + 1) * BLK],
                    fetched.at[slot, p, g],
                )
                for g in range(GROUP)
                for p in range(shares)
            ]

        for ahead in range(SLOTS - 1):

            @pl.when(ahead < steps)
            def _(ahead=ahead):
                for copy in fetch(ahead, ahead):
                    copy.start()

        moves = [pltpu.make_async_copy(source_any[i], source_refs[i], arrived.at[i]) for i in range(count)]
        for move in moves:
            move.start()
        for product in out_refs:
            product[...] = jnp.zeros_like(product)
        for move in moves:
            move.wait()

        def times(left, other):
            return lax.dot_general(left, other, (((1,), (1,)), ((), ())), preferred_element_type=jnp.float32)

        def body(step, _):
            slot = lax.rem(step, SLOTS)
            later = step + SLOTS - 1

            @pl.when(later < steps)
            def _():
                for copy in fetch(later, lax.rem(later, SLOTS)):
                    copy.start()

            for g in range(GROUP):
                entry = step * GROUP + g
                for panel, at_ref in enumerate((one_ref, two_ref)):
                    spot = at_ref[entry]
                    keep = jnp.logical_and(spot >= 0, entry < size_ref[0])
                    for source, start, height in zip(source_refs, starts, widths):
                        row = panel * width + start
                        value = source[:, lanes(jnp.maximum(spot, 0))]
                        high, low = split(jnp.where(keep, value, 0.0))
                        right[row : row + height, g * BLK : (g + 1) * BLK] = high
                        right[2 * width + row : 2 * width + row + height, g * BLK : (g + 1) * BLK] = low
            for copy in fetch(step, slot):
                copy.wait()
            high, low = split(slots[slot])
            both = times(high, right[...])
            both = both[:, : 2 * width] + both[:, 2 * width :] + times(low, right[: 2 * width, :])
            for p, product in enumerate(out_refs):
                product[...] += both[p * half : (p + 1) * half]
            return 0

        lax.fori_loop(0, steps, body, 0)

    anywhere = pl.BlockSpec(memory_space=pl.ANY)
    product = jax.ShapeDtypeStruct((half, 2 * width), jnp.float32)
    where = jnp.reshape(side, (1,)).astype(jnp.int32)
    return pl.pallas_call(
        kernel,
        in_specs=[in_smem()] * 5 + [anywhere] * (1 + count),
        out_specs=[in_vmem()] * outs,
        out_shape=[product] * shares,
        scratch_shapes=[pltpu.VMEM(source.shape, jnp.float32) for source in sources]
        + [
            pltpu.VMEM((SLOTS, shares * half, depth), jnp.float32),
            pltpu.VMEM((4 * width, depth), BF16),
            pltpu.SemaphoreType.DMA((SLOTS, shares, GROUP)),
            pltpu.SemaphoreType.DMA((count,)),
        ],
        compiler_params=pltpu.CompilerParams(vmem_limit_bytes=VMEM_BYTES),
        cost_estimate=pl.CostEstimate(
            flops=3 * shares * half * total * width * 2 * 2,
            transcendentals=0,
            bytes_accessed=shares * half * total * 3,
        ),
        name="panel_product",
    )(where, size, block_list, at_one, at_two, known_inverse, *sources)


def fold(groups, matrix, before):
    arrays, firsts, heights = [], [], []
    for mine, arrived, sources in groups:
        arrays += [mine, arrived]
        firsts += [first for _, first in sources]
        heights.append([array.shape[0] for array, _ in sources])
    rows = arrays[0].shape[0]
    total = matrix.shape[0] // 2
    count = len(arrays)
    has = before is not None

    def kernel(first_ref, *refs):
        ins, matrix_ref, out_ref = refs[:count], refs[count], refs[-1]

        def times(left, other):
            return lax.dot_general(left, other, (((1,), (0,)), ((), ())), preferred_element_type=jnp.float32)

        value = refs[count + 1][...] if has else None
        entry = 0
        for index, widths in enumerate(heights):
            parts = [
                matrix_ref[pl.ds(pl.multiple_of(panel * total + first_ref[entry + i], 32), w), :]
                for panel in range(2)
                for i, w in enumerate(widths)
            ]
            entry += len(widths)
            big, small = split(jnp.concatenate(parts, axis=0))
            high, low = split(ins[2 * index][...] + ins[2 * index + 1][...])
            part = times(high, big) + times(high, small) + times(low, big)
            value = part if value is None else value + part
        out_ref[...] = value

    return pl.pallas_call(
        kernel,
        in_specs=[in_smem()] + [in_vmem()] * (count + 1 + has),
        out_specs=in_vmem(),
        out_shape=jax.ShapeDtypeStruct((rows, 2 * total), jnp.float32),
        compiler_params=pltpu.CompilerParams(vmem_limit_bytes=VMEM_BYTES),
        cost_estimate=pl.CostEstimate(
            flops=6 * rows * 2 * total * sum(a.shape[1] for a in arrays[::2]),
            transcendentals=0,
            bytes_accessed=8 * rows * total * 2,
        ),
        name="fold",
    )(jnp.stack(firsts).astype(jnp.int32), *arrays, matrix, *([before] if has else []))


def own_rows(pieces, is_owner, total):
    arrays, firsts, heights = [], [], []
    for own, arrived, sources in pieces:
        arrays += [own, arrived]
        firsts += [first for _, first in sources]
        heights.append([array.shape[0] for array, _ in sources])
    count = len(arrays)
    length = arrays[0].shape[1]

    def kernel(first_ref, *refs):
        ins, outs = refs[:count], refs[count:]
        entry = 0
        for index, widths in enumerate(heights):
            here, there = ins[2 * index], ins[2 * index + 1]
            row = 0
            for panel, out in enumerate(outs):
                for i, w in enumerate(widths):
                    value = jnp.where(first_ref[0] > 0, here[row : row + w, :], there[row : row + w, :])
                    out[pl.ds(pl.multiple_of(first_ref[1 + entry + i], 32), w), :] = value
                    row += w
            entry += len(widths)

    return pl.pallas_call(
        kernel,
        in_specs=[in_smem()] + [in_vmem()] * count,
        out_specs=[in_vmem()] * 2,
        out_shape=[jax.ShapeDtypeStruct((total, length), jnp.float32)] * 2,
        compiler_params=pltpu.CompilerParams(vmem_limit_bytes=VMEM_BYTES),
        cost_estimate=pl.CostEstimate(flops=0, transcendentals=0, bytes_accessed=12 * total * length),
        name="own_rows",
    )(jnp.stack([is_owner] + firsts).astype(jnp.int32), *arrays)


def pairs(count, bit):
    return [(i, i ^ bit) for i in range(count)]


def halves(value, dim, side):
    size = value.shape[dim] // 2
    return (
        lax.dynamic_slice_in_dim(value, side * size, size, dim),
        lax.dynamic_slice_in_dim(value, (1 - side) * size, size, dim),
    )


def summed(value, stages):
    kept = []
    for axis, bit, halve in stages:
        count = lax.axis_size(axis)
        side = lax.axis_index(axis) // bit % 2
        if halve:
            mine, theirs = halves(value, 1 if axis == "col" else 0, side)
        else:
            mine = theirs = value
        value = mine + lax.ppermute(theirs, axis, pairs(count, bit))
        if halve and axis == "row":
            kept.append((bit, side))
    for bit, side in reversed(kept):
        other = lax.ppermute(value, "row", pairs(lax.axis_size("row"), bit))
        value = jnp.where(
            side == 0, jnp.concatenate([value, other], axis=0), jnp.concatenate([other, value], axis=0)
        )
    return value


def ring_chip(position, chips):
    half = chips // 2
    return jnp.where(position < half, 2 * position, 2 * (chips - 1 - position) + 1)


def sparse(
    known_inverse,
    first_panel,
    second_panel,
    coupling,
    first_diag,
    second_diag,
    first_present,
    second_present,
    capacity,
):
    rows = lax.axis_size("row")
    row_index = lax.axis_index("row")
    col_index = lax.axis_index("col")
    band_rows, block_cols = known_inverse.shape
    width = first_panel.shape[1]
    total = coupling.shape[0]
    part_rows = band_rows // 2
    blocks = block_cols // BLK
    chips = rows // 2
    reach = chips // 2
    core = row_index % 2
    chip = row_index // 2
    position = jnp.where(chip % 2 == 0, chip // 2, chips - 1 - chip // 2)
    order = [2 * p for p in range(reach)] + [2 * p + 1 for p in reversed(range(reach))]

    own, block_list, at_one, at_two, by_one, by_two, size = present_rows(
        jnp.reshape(col_index * blocks, (1,)).astype(jnp.int32),
        first_present,
        second_present,
        first_panel.T,
        second_panel.T,
        capacity,
    )
    places = (block_list, at_one, at_two, size)
    owner = row_index * band_rows // block_cols
    band = row_index * band_rows % block_cols // BLK
    to_other = []
    for r in range(rows):
        o = r * band_rows // block_cols
        to_other.append((2 * r + o, 2 * r + 1 - o))
    ring = []
    for p in range(chips):
        ring.append((2 * order[p], 2 * order[(p + 1) % chips]))
        ring.append((2 * order[p] + 1, 2 * order[(p - 1) % chips] + 1))

    def swap(value):
        return lax.ppermute(value, "row", pairs(rows, 1))

    def start(distance):
        return 2 * width * ring_chip((position + distance) % chips, chips)

    identity = jnp.eye(total, dtype=jnp.float32)
    matrix = jnp.concatenate(
        [
            jnp.concatenate([-identity, coupling], axis=1),
            jnp.concatenate([jnp.zeros_like(identity), -identity], axis=1),
        ],
        axis=0,
    )

    other = swap(own)
    moving = jnp.where(core == 0, jnp.concatenate([own, other]), jnp.concatenate([other, own]))
    way = jnp.where(core == 0, -1, 1)
    products, pieces = [], []
    for distance in range(reach + 1):
        last = distance == reach
        if distance == 0:
            sources = [(moving, start(0))]
        elif last:
            shift = jnp.where(core == 0, 0, width)
            sources = [(moving, start(distance) + shift), (swap(moving), start(distance) + width - shift)]
        else:
            sources = [(moving, start(way * distance)), (swap(moving), start(-way * distance))]
        if not last:
            if distance + 1 == reach:
                moving = jnp.where(core == 0, moving[:width], moving[width:])
            moving = lax.ppermute(moving, "row", ring)
        arrays = [array for array, _ in sources]
        other_piece, own_piece = band_rows_of(arrays, by_one, by_two, band, col_index, part_rows)
        arrived_piece = lax.ppermute(other_piece, ("row", "col"), to_other)
        theirs, mine = panel_product(known_inverse, arrays, places, col_index)
        before = (products[-1][1],) if products else (matrix,)
        if last:
            theirs, *before = lax.optimization_barrier((theirs, *before))
        else:
            moving, theirs, arrived_piece, *before = lax.optimization_barrier((moving, theirs, arrived_piece, *before))
        if products:
            products[-1] = (products[-1][0], before[0], products[-1][2])
        else:
            matrix = before[0]
        arrived = lax.ppermute(theirs, "col", pairs(2, 1))
        products.append((mine, arrived, sources))
        pieces.append((own_piece, arrived_piece, sources))

    blocks_out = fold(products[-1:], matrix, fold(products[:-1], matrix, None))
    first_block, second_block = blocks_out[:, :total], blocks_out[:, total:]
    rows_one, rows_two = own_rows(pieces, (col_index == owner).astype(jnp.int32), total)
    rows_two = rows_two - near(coupling, rows_one, (((0,), (0,)), ((), ())))
    sums = (-near(rows_one, first_block), -near(rows_one, second_block), -near(rows_two, second_block))
    bits = []
    bit = 2
    while bit < rows:
        bits.append(bit)
        bit *= 2
    cores, across = ("row", 1, True), ("col", 1, True)
    head, *rest = bits
    rest = [("row", b, False) for b in rest]
    turned = [("row", b, False) for b in bits[:1] + bits[2:]]
    ways = (
        [cores, across, ("row", head, True)] + rest,
        [cores, ("row", head, True), across] + rest,
        [cores, ("row", bits[1], True), across] + turned,
    )
    sums = [summed(value, way) for value, way in zip(sums, ways)]
    col_width = total // 2

    def own_columns(value):
        return lax.dynamic_slice_in_dim(value, col_index * col_width, col_width, 1)

    moved = near(first_diag, own_columns(coupling))
    first_out = own_columns(first_diag) + sums[0]
    cross_out = sums[1] - moved
    second_out = own_columns(second_diag) + near(coupling, moved, (((0,), (0,)), ((), ()))) + sums[2]
    return first_block, first_out, second_block, cross_out, second_out


def on_device(*args):
    known_inverse, first_panel, second_panel, coupling = args[:4]
    first_present, second_present = args[6:]
    rows, cols = lax.axis_size("row"), lax.axis_size("col")
    band_rows, block_cols = known_inverse.shape
    width = first_panel.shape[1]
    fits = (
        cols == 2
        and rows >= 4
        and rows & (rows - 1) == 0
        and band_rows % (2 * BLK) == 0
        and block_cols % (band_rows) == 0
        and block_cols % (GROUP * BLK) == 0
        and width % 32 == 0
        and coupling.shape[0] % (2 * 16 * rows) == 0
    )
    if not fits:
        return dense(*args)
    blocks = block_cols // BLK
    counts = (first_present + second_present).reshape(cols, blocks).sum(axis=1)
    capacities = [int(share * 2 * blocks) for share in LEVELS]
    level = sum((jnp.max(counts) > capacity).astype(jnp.int32) for capacity in capacities[:-1])
    branches = [functools.partial(sparse, capacity=capacity) for capacity in capacities]
    return lax.switch(level, branches, *args)


def solution(mesh):
    in_specs = (P("row", "col"), P("col", "row"), P("col", "row"), P(), P(), P(), P(), P())
    out_specs = (
        P(("row", "col"), None),
        P(None, "col"),
        P(("row", "col"), None),
        P(None, "col"),
        P(None, "col"),
    )
    return jax.shard_map(
        on_device, mesh=mesh, in_specs=in_specs, out_specs=out_specs, check_vma=False
    )
```

```python
import functools

import jax
import jax.numpy as jnp
from jax import lax
from jax.experimental import pallas as pl
from jax.experimental.pallas import tpu as pltpu
from jax.sharding import PartitionSpec as P

BLK = 128
GROUP = 4
SLOTS = 3
VMEM_BYTES = 50 * 2**20
LEVELS = (0.55, 0.6, 1.0)
BF16 = jnp.bfloat16


def product(left, right):
    return jnp.dot(left, right, precision=lax.Precision.HIGHEST, preferred_element_type=jnp.float32)


def transposed(left, right):
    return lax.dot_general(
        left,
        right,
        (((0,), (0,)), ((), ())),
        precision=lax.Precision.HIGHEST,
        preferred_element_type=jnp.float32,
    )


def masked(panel, present, col_index):
    row_total, col_total = panel.shape
    blocks = row_total // BLK
    local = lax.dynamic_slice_in_dim(present, col_index * blocks, blocks)
    shaped = panel.reshape(blocks, BLK, col_total) * local.astype(jnp.float32)[:, None, None]
    return shaped.reshape(row_total, col_total)


def piece_products(known_inverse, column_one, column_two, piece_one, piece_two, coupling):
    first_block = -lax.psum_scatter(
        product(known_inverse, column_one), "col", scatter_dimension=0, tiled=True
    )
    reached = lax.psum_scatter(
        product(known_inverse, column_two), "col", scatter_dimension=0, tiled=True
    )
    first_partial = transposed(piece_one, first_block)
    second_block = -(reached + product(first_block, coupling))
    cross_partial = transposed(first_block, piece_two)
    diag_partial = transposed(piece_two, second_block)
    return (first_block, second_block, first_partial, cross_partial, diag_partial)


def dense(
    known_inverse,
    first_panel,
    second_panel,
    coupling,
    first_diag,
    second_diag,
    first_present,
    second_present,
):
    col_count = lax.axis_size("col")
    row_index = lax.axis_index("row")
    col_index = lax.axis_index("col")
    local_one = masked(first_panel, first_present, col_index)
    local_two = masked(second_panel, second_present, col_index)
    column_one, column_two = (
        lax.all_gather(local_one, "row", axis=1, tiled=True),
        lax.all_gather(local_two, "row", axis=1, tiled=True),
    )
    band_rows = known_inverse.shape[0]
    block_cols = known_inverse.shape[1]
    width_total = coupling.shape[0]
    owner = row_index * band_rows // block_cols
    offset = row_index * band_rows % block_cols
    is_owner = (col_index == owner).astype(jnp.float32)
    band_one = lax.dynamic_slice_in_dim(column_one, offset, band_rows) * is_owner
    band_two = lax.dynamic_slice_in_dim(column_two, offset, band_rows) * is_owner
    piece_one, piece_two = (
        lax.psum_scatter(band_one, "col", scatter_dimension=0, tiled=True),
        lax.psum_scatter(band_two, "col", scatter_dimension=0, tiled=True),
    )
    first_block, second_block, first_partial, cross_partial, diag_partial = piece_products(
        known_inverse, column_one, column_two, piece_one, piece_two, coupling
    )
    col_width = width_total // col_count
    col_start = col_index * col_width
    first_sum = lax.psum(first_partial, ("row", "col"))
    first_inverse_diag = first_diag - first_sum
    cross_sum, diag_sum = lax.psum((cross_partial, diag_partial), ("row", "col"))
    second_cross = -(cross_sum + product(first_inverse_diag, coupling))
    second_inverse_diag = second_diag - diag_sum - transposed(coupling, second_cross)
    first_out = lax.dynamic_slice_in_dim(first_inverse_diag, col_start, col_width, 1)
    cross_out = lax.dynamic_slice_in_dim(second_cross, col_start, col_width, 1)
    second_out = lax.dynamic_slice_in_dim(second_inverse_diag, col_start, col_width, 1)
    return (first_block, first_out, second_block, cross_out, second_out)


def near(left, right, dims=(((1,), (0,)), ((), ()))):
    return lax.dot_general(left, right, dims, precision=lax.Precision.HIGH, preferred_element_type=jnp.float32)


def in_smem():
    return pl.BlockSpec(memory_space=pltpu.SMEM)


def in_vmem():
    return pl.BlockSpec(memory_space=pltpu.VMEM)


def lanes(start):
    return pl.ds(pl.multiple_of(start * BLK, BLK), BLK)


def split(value):
    high = value.astype(BF16)
    return high, (value - high.astype(jnp.float32)).astype(BF16)


def present_rows(first, one, two, panel_one, panel_two, capacity):
    width, total = panel_one.shape
    blocks = total // BLK

    def kernel(at_ref, one_ref, two_ref, first_ref, second_ref, out_ref, list_ref, at_one, at_two, by_one, by_two, size_ref):
        def body(block, carry):
            place = carry
            for present_ref, source, by_ref in (
                (one_ref, first_ref, by_one),
                (two_ref, second_ref, by_two),
            ):
                here = present_ref[at_ref[0] + block]
                spot = jnp.where(here > 0, place, -1)
                by_ref[block] = spot

                @pl.when(jnp.logical_and(here > 0, place < capacity))
                def _(place=place, source=source):
                    out_ref[:, lanes(place)] = source[:, lanes(block)]

                place = place + here
            return place

        place = lax.fori_loop(0, blocks, body, jnp.int32(0))

        def listed(block, size, kind):
            here = (by_one[block] >= 0, by_two[block] >= 0)
            found = jnp.logical_and(here[0] == (kind != 2), here[1] == (kind != 1))

            @pl.when(found)
            def _():
                list_ref[size] = block
                at_one[size] = by_one[block]
                at_two[size] = by_two[block]

            return size + found.astype(jnp.int32)

        size = jnp.int32(0)
        for kind in range(3):
            size = lax.fori_loop(0, blocks, lambda block, size, kind=kind: listed(block, size, kind), size)
        size_ref[0] = size

        def rest(entry, _):
            list_ref[entry] = 0
            at_one[entry] = -1
            at_two[entry] = -1
            return 0

        lax.fori_loop(size, blocks, rest, 0)

        def clear(entry, _):
            out_ref[:, lanes(entry)] = jnp.zeros((width, BLK), jnp.float32)
            return 0

        lax.fori_loop(jnp.minimum(place, capacity), capacity, clear, 0)

    ints = jax.ShapeDtypeStruct((blocks,), jnp.int32)
    return pl.pallas_call(
        kernel,
        in_specs=[in_smem()] * 3 + [in_vmem()] * 2,
        out_specs=[in_vmem()] + [in_smem()] * 6,
        out_shape=[
            jax.ShapeDtypeStruct((width, capacity * BLK), jnp.float32),
            ints,
            ints,
            ints,
            ints,
            ints,
            jax.ShapeDtypeStruct((1,), jnp.int32),
        ],
        compiler_params=pltpu.CompilerParams(vmem_limit_bytes=VMEM_BYTES),
        cost_estimate=pl.CostEstimate(flops=0, transcendentals=0, bytes_accessed=20 * 2**20),
        name="present_rows",
    )(first, one, two, panel_one, panel_two)


def band_rows_of(sources, by_one, by_two, band, side, half):
    widths = [source.shape[0] for source in sources]
    width = sum(widths)
    starts = [sum(widths[:i]) for i in range(len(widths))]
    count = len(sources)

    def kernel(where_ref, one_ref, two_ref, *refs):
        ins, outs = refs[:count], refs[count:]
        parts = (1 - where_ref[0], where_ref[0])
        for panel, by_ref in enumerate((one_ref, two_ref)):
            for p, out in enumerate(outs):
                for block in range(half // BLK):
                    spot = by_ref[where_ref[1] + parts[p] * (half // BLK) + block]
                    for source, start, height in zip(ins, starts, widths):
                        row = panel * width + start
                        value = source[:, lanes(jnp.maximum(spot, 0))]
                        out[row : row + height, block * BLK : (block + 1) * BLK] = jnp.where(spot >= 0, value, 0.0)

    return pl.pallas_call(
        kernel,
        in_specs=[in_smem()] * 3 + [in_vmem()] * count,
        out_specs=[in_vmem()] * 2,
        out_shape=[jax.ShapeDtypeStruct((2 * width, half), jnp.float32)] * 2,
        compiler_params=pltpu.CompilerParams(vmem_limit_bytes=VMEM_BYTES),
        cost_estimate=pl.CostEstimate(flops=0, transcendentals=0, bytes_accessed=10 * 2**20),
        name="band_rows",
    )(jnp.stack([side, band]).astype(jnp.int32), by_one, by_two, *sources)


def panel_product(known_inverse, sources, places, side):
    block_list, at_one, at_two, size = places
    rows, total = known_inverse.shape
    half = rows // 2
    shares = 2
    widths = [source.shape[0] for source in sources]
    width = sum(widths)
    starts = [sum(widths[:i]) for i in range(len(widths))]
    depth = GROUP * BLK
    count = len(sources)
    outs = shares

    def kernel(where_ref, size_ref, list_ref, one_ref, two_ref, known_ref, *refs):
        source_any, out_refs = refs[:count], refs[count : count + outs]
        source_refs = refs[count + outs : 2 * count + outs]
        slots, right, fetched, arrived = refs[2 * count + outs :]
        steps = (size_ref[0] + GROUP - 1) // GROUP
        parts = (1 - where_ref[0], where_ref[0])

        def fetch(step, slot):
            return [
                pltpu.make_async_copy(
                    known_ref.at[pl.ds(pl.multiple_of(parts[p] * half, half), half), lanes(list_ref[step * GROUP + g])],
                    slots.at[slot, p * half : (p + 1) * half, g * BLK : (g + 1) * BLK],
                    fetched.at[slot, p, g],
                )
                for g in range(GROUP)
                for p in range(shares)
            ]

        for ahead in range(SLOTS - 1):

            @pl.when(ahead < steps)
            def _(ahead=ahead):
                for copy in fetch(ahead, ahead):
                    copy.start()

        moves = [pltpu.make_async_copy(source_any[i], source_refs[i], arrived.at[i]) for i in range(count)]
        for move in moves:
            move.start()
        for product in out_refs:
            product[...] = jnp.zeros_like(product)
        for move in moves:
            move.wait()

        def times(left, other):
            return lax.dot_general(left, other, (((1,), (1,)), ((), ())), preferred_element_type=jnp.float32)

        def body(step, _):
            slot = lax.rem(step, SLOTS)
            later = step + SLOTS - 1

            @pl.when(later < steps)
            def _():
                for copy in fetch(later, lax.rem(later, SLOTS)):
                    copy.start()

            for g in range(GROUP):
                entry = step * GROUP + g
                for panel, at_ref in enumerate((one_ref, two_ref)):
                    spot = at_ref[entry]
                    keep = jnp.logical_and(spot >= 0, entry < size_ref[0])
                    for source, start, height in zip(source_refs, starts, widths):
                        row = panel * width + start
                        value = source[:, lanes(jnp.maximum(spot, 0))]
                        high, low = split(jnp.where(keep, value, 0.0))
                        right[row : row + height, g * BLK : (g + 1) * BLK] = high
                        right[2 * width + row : 2 * width + row + height, g * BLK : (g + 1) * BLK] = low
            for copy in fetch(step, slot):
                copy.wait()

            def add(first, last):
                high, low = split(slots[slot])
                big, small = right[first:last, :], right[2 * width + first : 2 * width + last, :]
                both = times(high, jnp.concatenate([big, small], axis=0))
                both = both[:, : last - first] + both[:, last - first :] + times(low, big)
                for p, product in enumerate(out_refs):
                    product[:, first:last] += both[p * half : (p + 1) * half]

            if width % BLK:
                add(0, 2 * width)
            else:
                has_one, has_two = False, False
                for g in range(GROUP):
                    has_one = jnp.logical_or(has_one, one_ref[step * GROUP + g] >= 0)
                    has_two = jnp.logical_or(has_two, two_ref[step * GROUP + g] >= 0)
                pl.when(jnp.logical_and(has_one, has_two))(lambda: add(0, 2 * width))
                pl.when(jnp.logical_and(has_one, jnp.logical_not(has_two)))(lambda: add(0, width))
                pl.when(jnp.logical_and(has_two, jnp.logical_not(has_one)))(lambda: add(width, 2 * width))
            return 0

        lax.fori_loop(0, steps, body, 0)

    anywhere = pl.BlockSpec(memory_space=pl.ANY)
    product = jax.ShapeDtypeStruct((half, 2 * width), jnp.float32)
    where = jnp.reshape(side, (1,)).astype(jnp.int32)
    return pl.pallas_call(
        kernel,
        in_specs=[in_smem()] * 5 + [anywhere] * (1 + count),
        out_specs=[in_vmem()] * outs,
        out_shape=[product] * shares,
        scratch_shapes=[pltpu.VMEM(source.shape, jnp.float32) for source in sources]
        + [
            pltpu.VMEM((SLOTS, shares * half, depth), jnp.float32),
            pltpu.VMEM((4 * width, depth), BF16),
            pltpu.SemaphoreType.DMA((SLOTS, shares, GROUP)),
            pltpu.SemaphoreType.DMA((count,)),
        ],
        compiler_params=pltpu.CompilerParams(vmem_limit_bytes=VMEM_BYTES),
        cost_estimate=pl.CostEstimate(
            flops=3 * shares * half * total * width * 2 * 2,
            transcendentals=0,
            bytes_accessed=shares * half * total * 3,
        ),
        name="panel_product",
    )(where, size, block_list, at_one, at_two, known_inverse, *sources)


def fold(groups, matrix, before):
    arrays, firsts, heights = [], [], []
    for mine, arrived, sources in groups:
        arrays += [mine, arrived]
        firsts += [first for _, first in sources]
        heights.append([array.shape[0] for array, _ in sources])
    rows = arrays[0].shape[0]
    total = matrix.shape[0] // 2
    count = len(arrays)
    has = before is not None

    def kernel(first_ref, *refs):
        ins, matrix_ref, out_ref = refs[:count], refs[count], refs[-1]

        def times(left, other):
            return lax.dot_general(left, other, (((1,), (0,)), ((), ())), preferred_element_type=jnp.float32)

        value = refs[count + 1][...] if has else None
        entry = 0
        for index, widths in enumerate(heights):
            parts = [
                matrix_ref[pl.ds(pl.multiple_of(panel * total + first_ref[entry + i], 32), w), :]
                for panel in range(2)
                for i, w in enumerate(widths)
            ]
            entry += len(widths)
            big, small = split(jnp.concatenate(parts, axis=0))
            high, low = split(ins[2 * index][...] + ins[2 * index + 1][...])
            part = times(high, big) + times(high, small) + times(low, big)
            value = part if value is None else value + part
        out_ref[...] = value

    return pl.pallas_call(
        kernel,
        in_specs=[in_smem()] + [in_vmem()] * (count + 1 + has),
        out_specs=in_vmem(),
        out_shape=jax.ShapeDtypeStruct((rows, 2 * total), jnp.float32),
        compiler_params=pltpu.CompilerParams(vmem_limit_bytes=VMEM_BYTES),
        cost_estimate=pl.CostEstimate(
            flops=6 * rows * 2 * total * sum(a.shape[1] for a in arrays[::2]),
            transcendentals=0,
            bytes_accessed=8 * rows * total * 2,
        ),
        name="fold",
    )(jnp.stack(firsts).astype(jnp.int32), *arrays, matrix, *([before] if has else []))


def own_rows(pieces, is_owner, total):
    arrays, firsts, heights = [], [], []
    for own, arrived, sources in pieces:
        arrays += [own, arrived]
        firsts += [first for _, first in sources]
        heights.append([array.shape[0] for array, _ in sources])
    count = len(arrays)
    length = arrays[0].shape[1]

    def kernel(first_ref, *refs):
        ins, outs = refs[:count], refs[count:]
        entry = 0
        for index, widths in enumerate(heights):
            here, there = ins[2 * index], ins[2 * index + 1]
            row = 0
            for panel, out in enumerate(outs):
                for i, w in enumerate(widths):
                    value = jnp.where(first_ref[0] > 0, here[row : row + w, :], there[row : row + w, :])
                    out[pl.ds(pl.multiple_of(first_ref[1 + entry + i], 32), w), :] = value
                    row += w
            entry += len(widths)

    return pl.pallas_call(
        kernel,
        in_specs=[in_smem()] + [in_vmem()] * count,
        out_specs=[in_vmem()] * 2,
        out_shape=[jax.ShapeDtypeStruct((total, length), jnp.float32)] * 2,
        compiler_params=pltpu.CompilerParams(vmem_limit_bytes=VMEM_BYTES),
        cost_estimate=pl.CostEstimate(flops=0, transcendentals=0, bytes_accessed=12 * total * length),
        name="own_rows",
    )(jnp.stack([is_owner] + firsts).astype(jnp.int32), *arrays)


def pairs(count, bit):
    return [(i, i ^ bit) for i in range(count)]


def halves(value, dim, side):
    size = value.shape[dim] // 2
    return (
        lax.dynamic_slice_in_dim(value, side * size, size, dim),
        lax.dynamic_slice_in_dim(value, (1 - side) * size, size, dim),
    )


def summed(value, stages):
    kept = []
    for axis, bit, halve in stages:
        count = lax.axis_size(axis)
        side = lax.axis_index(axis) // bit % 2
        if halve:
            mine, theirs = halves(value, 1 if axis == "col" else 0, side)
        else:
            mine = theirs = value
        value = mine + lax.ppermute(theirs, axis, pairs(count, bit))
        if halve and axis == "row":
            kept.append((bit, side))
    for bit, side in reversed(kept):
        other = lax.ppermute(value, "row", pairs(lax.axis_size("row"), bit))
        value = jnp.where(
            side == 0, jnp.concatenate([value, other], axis=0), jnp.concatenate([other, value], axis=0)
        )
    return value


def ring_chip(position, chips):
    half = chips // 2
    return jnp.where(position < half, 2 * position, 2 * (chips - 1 - position) + 1)


def sparse(
    known_inverse,
    first_panel,
    second_panel,
    coupling,
    first_diag,
    second_diag,
    first_present,
    second_present,
    capacity,
):
    rows = lax.axis_size("row")
    row_index = lax.axis_index("row")
    col_index = lax.axis_index("col")
    band_rows, block_cols = known_inverse.shape
    width = first_panel.shape[1]
    total = coupling.shape[0]
    part_rows = band_rows // 2
    blocks = block_cols // BLK
    chips = rows // 2
    reach = chips // 2
    core = row_index % 2
    chip = row_index // 2
    position = jnp.where(chip % 2 == 0, chip // 2, chips - 1 - chip // 2)
    order = [2 * p for p in range(reach)] + [2 * p + 1 for p in reversed(range(reach))]

    own, block_list, at_one, at_two, by_one, by_two, size = present_rows(
        jnp.reshape(col_index * blocks, (1,)).astype(jnp.int32),
        first_present,
        second_present,
        first_panel.T,
        second_panel.T,
        capacity,
    )
    places = (block_list, at_one, at_two, size)
    owner = row_index * band_rows // block_cols
    band = row_index * band_rows % block_cols // BLK
    to_other = []
    for r in range(rows):
        o = r * band_rows // block_cols
        to_other.append((2 * r + o, 2 * r + 1 - o))
    ring = []
    for p in range(chips):
        ring.append((2 * order[p], 2 * order[(p + 1) % chips]))
        ring.append((2 * order[p] + 1, 2 * order[(p - 1) % chips] + 1))

    def swap(value):
        return lax.ppermute(value, "row", pairs(rows, 1))

    def start(distance):
        return 2 * width * ring_chip((position + distance) % chips, chips)

    identity = jnp.eye(total, dtype=jnp.float32)
    matrix = jnp.concatenate(
        [
            jnp.concatenate([-identity, coupling], axis=1),
            jnp.concatenate([jnp.zeros_like(identity), -identity], axis=1),
        ],
        axis=0,
    )

    other = swap(own)
    moving = jnp.where(core == 0, jnp.concatenate([own, other]), jnp.concatenate([other, own]))
    way = jnp.where(core == 0, -1, 1)
    products, pieces = [], []
    for distance in range(reach + 1):
        last = distance == reach
        if distance == 0:
            sources = [(moving, start(0))]
        elif last:
            shift = jnp.where(core == 0, 0, width)
            sources = [(moving, start(distance) + shift), (swap(moving), start(distance) + width - shift)]
        else:
            sources = [(moving, start(way * distance)), (swap(moving), start(-way * distance))]
        if not last:
            if distance + 1 == reach:
                moving = jnp.where(core == 0, moving[:width], moving[width:])
            moving = lax.ppermute(moving, "row", ring)
        arrays = [array for array, _ in sources]
        other_piece, own_piece = band_rows_of(arrays, by_one, by_two, band, col_index, part_rows)
        arrived_piece = lax.ppermute(other_piece, ("row", "col"), to_other)
        theirs, mine = panel_product(known_inverse, arrays, places, col_index)
        before = (products[-1][1],) if products else (matrix,)
        if last:
            theirs, *before = lax.optimization_barrier((theirs, *before))
        else:
            moving, theirs, arrived_piece, *before = lax.optimization_barrier((moving, theirs, arrived_piece, *before))
        if products:
            products[-1] = (products[-1][0], before[0], products[-1][2])
        else:
            matrix = before[0]
        arrived = lax.ppermute(theirs, "col", pairs(2, 1))
        products.append((mine, arrived, sources))
        pieces.append((own_piece, arrived_piece, sources))

    blocks_out = fold(products[-1:], matrix, fold(products[:-1], matrix, None))
    first_block, second_block = blocks_out[:, :total], blocks_out[:, total:]
    rows_one, rows_two = own_rows(pieces, (col_index == owner).astype(jnp.int32), total)
    rows_two = rows_two - near(coupling, rows_one, (((0,), (0,)), ((), ())))
    sums = (-near(rows_one, first_block), -near(rows_one, second_block), -near(rows_two, second_block))
    bits = []
    bit = 2
    while bit < rows:
        bits.append(bit)
        bit *= 2
    cores, across = ("row", 1, True), ("col", 1, True)
    head, *rest = bits
    rest = [("row", b, False) for b in rest]
    turned = [("row", b, False) for b in bits[:1] + bits[2:]]
    ways = (
        [cores, across, ("row", head, True)] + rest,
        [cores, ("row", head, True), across] + rest,
        [cores, ("row", bits[1], True), across] + turned,
    )
    sums = [summed(value, way) for value, way in zip(sums, ways)]
    col_width = total // 2

    def own_columns(value):
        return lax.dynamic_slice_in_dim(value, col_index * col_width, col_width, 1)

    moved = near(first_diag, own_columns(coupling))
    first_out = own_columns(first_diag) + sums[0]
    cross_out = sums[1] - moved
    second_out = own_columns(second_diag) + near(coupling, moved, (((0,), (0,)), ((), ()))) + sums[2]
    return first_block, first_out, second_block, cross_out, second_out


def on_device(*args):
    known_inverse, first_panel, second_panel, coupling = args[:4]
    first_present, second_present = args[6:]
    rows, cols = lax.axis_size("row"), lax.axis_size("col")
    band_rows, block_cols = known_inverse.shape
    width = first_panel.shape[1]
    fits = (
        cols == 2
        and rows >= 4
        and rows & (rows - 1) == 0
        and band_rows % (2 * BLK) == 0
        and block_cols % (band_rows) == 0
        and block_cols % (GROUP * BLK) == 0
        and width % 32 == 0
        and coupling.shape[0] % (2 * 16 * rows) == 0
    )
    if not fits:
        return dense(*args)
    blocks = block_cols // BLK
    counts = (first_present + second_present).reshape(cols, blocks).sum(axis=1)
    capacities = [int(share * 2 * blocks) for share in LEVELS]
    level = sum((jnp.max(counts) > capacity).astype(jnp.int32) for capacity in capacities[:-1])
    branches = [functools.partial(sparse, capacity=capacity) for capacity in capacities]
    return lax.switch(level, branches, *args)


def solution(mesh):
    in_specs = (P("row", "col"), P("col", "row"), P("col", "row"), P(), P(), P(), P(), P())
    out_specs = (
        P(("row", "col"), None),
        P(None, "col"),
        P(("row", "col"), None),
        P(None, "col"),
        P(None, "col"),
    )
    return jax.shard_map(
        on_device, mesh=mesh, in_specs=in_specs, out_specs=out_specs, check_vma=False
    )
```
